32 devices in a mesh: groups: 2 (over y), dp: 4 (over z), tensor: 2 (over x), sub: 2 (over core).
Axes of the slice: x: 2, y: 2, z: 4, core: 2. Of those that a mesh axis runs over, the one named last changes fastest.
Arguments:
- acts: bfloat16 [2, 8192, 14336], P(None, ('groups', 'dp'), ('tensor', 'sub')), parts along dimension 1, may hold values from -6 to 6
- grads_out: bfloat16 [2, 8192, 4096], P(None, ('groups', 'dp'), ('tensor', 'sub')), parts along dimension 1, may hold values from -6 to 6
- lengths: int32 [16], P(('groups', 'dp')), parts along dimension 0, may hold values from 128 to 512
- proj_in: bfloat16 [2, 14336, 64], P(None, ('tensor', 'sub')), may hold values from -0.046875 to 0.046875
- proj_out: bfloat16 [2, 4096, 64], P(None, ('tensor', 'sub')), may hold values from -0.09375 to 0.09375
- query_grads: bfloat16 [256, 8192], P('dp', ('tensor', 'sub')), may hold values from -0.0625 to 0.0625
Outputs:
- sketches: float32 [16, 8192], P(('groups', 'dp'), ('tensor', 'sub')), parts along dimension 0
- scores: float32 [256, 16], P(None, ('groups', 'dp')), parts along dimension 1
The draws below stay inside these ranges and needn't reach their ends.
There are 2 independent parts, one for each index of `groups`. The reference program is written for one: setup_inputs(seed, part) draws one part's arguments, and reference() takes and returns one part's arrays. A program takes and returns all parts, laid end to end along the dimension named above; an argument that names none is the same for every part. Nothing has to cross between parts.
Inputs may be any that keep to these rules, and one draw needn't show every extreme that they name: The live tokens of a sequence are its first lengths[e] slots.
All inputs are finite; a program needn't handle non-finite values.
Results may differ from the reference program's by a relative error of at most 0.0003.
Values may be sent and summed in bfloat16 or wider, within the bound.
A program may use at most 64 MiB of HBM per device.

```python
import jax
import jax.numpy as jnp
from jax import lax

D = 4096
FF = 14336
K = 64
LAYERS = 2
SEQ_LEN = 512
TOKENS = 4096
EXAMPLES = 8
QUERIES = 256
FEATS = 8192


def set_ends(result, stream_key, least, largest):
    longest = result.shape.index(max(result.shape))
    spots = []
    for shift in (0, 1):
        where = [jax.random.randint(jax.random.fold_in(stream_key, axis), (), 0, length) for axis, length in enumerate(result.shape)]
        where[longest] = (where[longest] + shift) % result.shape[longest]
        spots.append(tuple(where))
    return result.at[spots[0]].set(least).at[spots[1]].set(largest)


def shard_levels(rng, extent, pieces, low, high):
    loudness = 1.0
    for dim, parts in pieces:
        draws = jax.random.uniform(jax.random.fold_in(jax.random.fold_in(rng, 6), dim), (parts,), jnp.float32, low / len(pieces), high / len(pieces))
        loudness = loudness * jnp.repeat(jnp.exp(draws), extent[dim] // parts).reshape((-1,) + (1,) * (len(extent) - 1 - dim))
    return loudness


def noise(rng, extent, deviation, reach, shards=(), kind=jnp.bfloat16):
    drawn = jax.random.normal(rng, extent, jnp.float32) * deviation
    if len(shards) > 0:
        drawn = shard_levels(rng, extent, shards, -0.22, 0.18) * drawn
    return jnp.clip(drawn, min=-reach, max=reach).astype(kind)


def setup_inputs(seed: int = 0, part: int = 0) -> dict:
    key_of = jax.random.split(jax.random.key(seed), 7)
    part_keys = jax.random.split(jax.random.fold_in(key_of[6], part), 7)
    return {
        "acts": noise(part_keys[0], (LAYERS, TOKENS, FF), 1.0, 6.0, ((1, 4), (2, 4))),
        "grads_out": noise(part_keys[1], (LAYERS, TOKENS, D), 1.0, 6.0, ((1, 4), (2, 4))),
        "lengths": set_ends(jax.random.randint(part_keys[2], (EXAMPLES,), SEQ_LEN // 4, SEQ_LEN + 1), jax.random.fold_in(part_keys[2], 1), SEQ_LEN // 4, SEQ_LEN).astype(jnp.int32),
        "proj_in": noise(key_of[3], (LAYERS, FF, K), FF ** -0.5, 0.046875, ((1, 4),)),
        "proj_out": noise(key_of[4], (LAYERS, D, K), D ** -0.5, 0.09375, ((1, 4),)),
        "query_grads": noise(key_of[5], (QUERIES, FEATS), FEATS ** -0.5, 0.0625, ((0, 4), (1, 4))),
    }


def reference(acts, grads_out, lengths, proj_in, proj_out, query_grads):
    proj_a = jnp.stack([jnp.dot(acts[layer], proj_in[layer], preferred_element_type=jnp.float32) for layer in range(LAYERS)], axis=1)
    proj_b = jnp.stack([jnp.dot(grads_out[layer], proj_out[layer], preferred_element_type=jnp.float32) for layer in range(LAYERS)], axis=1)
    slots = jnp.arange(SEQ_LEN, dtype=jnp.int32)
    live = (slots[None, :] < lengths[:, None]).astype(jnp.float32)
    proj_a = proj_a.reshape(EXAMPLES, SEQ_LEN, LAYERS, K) * live[:, :, None, None]
    proj_b = proj_b.reshape(EXAMPLES, SEQ_LEN, LAYERS, K)
    sketch = jnp.einsum("esli,eslj->elij", proj_a, proj_b, precision=lax.Precision.HIGHEST)
    sketches = (sketch * (SEQ_LEN ** -0.5)).reshape(EXAMPLES, FEATS)
    scores = jnp.dot(query_grads.astype(jnp.float32), sketches.T, precision=lax.Precision.HIGHEST)
    return sketches, scores
```

```python
import functools
import jax
import jax.numpy as jnp
from jax import lax
from jax.experimental import pallas as pl
from jax.experimental.pallas import tpu as pltpu
from jax.sharding import PartitionSpec as P

SEQ_LEN = 512
LANES = 128
MESH = pl.DeviceIdType.MESH
NT = (((1,), (1,)), ((), ()))


def project_side(inputs, weights):
    return jnp.concatenate(
        [
            jnp.dot(inputs[layer], weights[layer], preferred_element_type=jnp.float32)
            for layer in range(inputs.shape[0])
        ],
        axis=1,
    )


def sketch_terms(side_a, side_b, weights, layers):
    rows = side_a.shape[0]
    width = side_a.shape[1] // layers
    left = side_a.reshape(rows, layers, width)
    right = side_b.reshape(rows, layers, width)
    result = jnp.einsum("te,tli,tlj->elij", weights, left, right, precision=lax.Precision.HIGHEST)
    return (result * SEQ_LEN ** (-0.5)).reshape(weights.shape[1], layers * width * width)


def row_weights(lengths, rows, seq_len):
    token = jnp.arange(rows, dtype=jnp.int32)
    seq_of = token // seq_len
    slot = token % seq_len
    owners = jnp.arange(lengths.shape[0], dtype=jnp.int32)
    match = seq_of[:, None] == owners[None, :]
    bound = jnp.sum(jnp.where(match, lengths[None, :], 0), axis=1)
    live = (slot < bound).astype(jnp.float32)
    return match.astype(jnp.float32) * live[:, None]


def per_device(acts, grads_out, lengths, proj_in, proj_out, query_grads):
    layers, rows, _ = acts.shape
    seqs = lengths.shape[0]
    seq_len = rows // seqs
    side_a = project_side(acts, proj_in)
    side_b = project_side(grads_out, proj_out)
    count = lax.axis_size(("tensor", "sub"))
    rank = lax.axis_index(("tensor", "sub"))
    feats = layers * proj_in.shape[2] * proj_in.shape[2]
    share = feats // count
    whole_a, whole_b = lax.psum((side_a, side_b), ("tensor", "sub"))
    weights = row_weights(lengths, rows, seq_len)
    full_sketch = sketch_terms(whole_a, whole_b, weights, layers)
    mine = lax.dynamic_slice_in_dim(full_sketch, rank * share, share, 1)
    block = jnp.dot(
        lax.all_gather(query_grads, "dp", axis=0, tiled=True).astype(jnp.float32),
        mine.T,
        precision=lax.Precision.HIGHEST,
    )
    scores = lax.psum(block, ("tensor", "sub"))
    return (mine, scores)


def kernel(
    dps, chunk, steps,
    x_hbm, g_hbm, len_ref, w_hbm, v_hbm, q_hbm,
    sk_ref, sc_ref,
    x, g, w, v, q, away, mine, sub_in, ten_in, tab, flat_ref, all_sk, wide, snd, rcv,
    x_sem, g_sem, w_sem, v_sem, q_sem,
    sub_s, sub_r, ten_s, ten_r, sk_s, sk_r, sc_s, sc_r,
):
    d = lax.axis_index("dp")
    t = lax.axis_index("tensor")
    c = lax.axis_index("sub")
    ot, oc = 1 - t, 1 - c
    k = w.shape[1]
    seq_len = SEQ_LEN

    items = []
    for layer in (ot, t):
        for part in range(steps):
            for half in (oc, c):
                items.append((layer, half * seq_len + part * chunk))

    def fetch_w(n, layer):
        return (
            pltpu.make_async_copy(w_hbm.at[layer], w.at[layer], w_sem.at[n]),
            pltpu.make_async_copy(v_hbm.at[layer], v.at[layer], v_sem.at[n]),
        )

    def fetch(n):
        layer, row = items[n]
        at = pl.ds(pl.multiple_of(row, chunk), chunk)
        return (
            pltpu.make_async_copy(x_hbm.at[layer, at], x.at[layer, at], x_sem.at[n]),
            pltpu.make_async_copy(g_hbm.at[layer, at], g.at[layer, at], g_sem.at[n]),
        )

    loads = []
    weight_loads = [fetch_w(0, ot), fetch_w(1, t)]
    for n in range(len(items)):
        if n == 0 or n == len(items) // 2:
            for copy in weight_loads[0 if n == 0 else 1]:
                copy.start()
        loads.append(fetch(n))
        for copy in loads[-1]:
            copy.start()
    q_load = pltpu.make_async_copy(q_hbm, q, q_sem)
    q_load.start()

    others = []
    for a in range(dps):
        for b in range(2):
            for e in range(2):
                if a or b or e:
                    others.append((lax.rem(d + a, dps), lax.rem(t + b, 2), lax.rem(c + e, 2)))
    barrier = pltpu.get_barrier_semaphore()
    for dd, tt, cc in others:
        pl.semaphore_signal(
            barrier, inc=1, device_id={"dp": dd, "tensor": tt, "sub": cc}, device_id_type=MESH
        )

    def project(n, out):
        if n == 0 or n == len(items) // 2:
            for copy in weight_loads[0 if n == 0 else 1]:
                copy.wait()
        for copy in loads[n]:
            copy.wait()
        layer, row = items[n]
        at = pl.ds(pl.multiple_of(row, chunk), chunk)
        out[:, 0:k] = lax.dot_general(x[layer, at, :], w[layer], NT, preferred_element_type=jnp.float32)
        out[:, k : 2 * k] = lax.dot_general(g[layer, at, :], v[layer], NT, preferred_element_type=jnp.float32)

    sub_copies, ten_copies = [], []
    for s in range(2 * steps):
        project(2 * s, away.at[s])
        if s == 0:
            pl.semaphore_wait(barrier, len(others))
        copy = pltpu.make_async_remote_copy(
            src_ref=away.at[s], dst_ref=sub_in.at[s], send_sem=sub_s.at[s], recv_sem=sub_r.at[s],
            device_id={"sub": oc}, device_id_type=MESH,
        )
        copy.start()
        sub_copies.append(copy)
        project(2 * s + 1, mine.at[s])
        copy.wait_recv()
        mine[s] += sub_in[s]
        if s < steps:
            copy = pltpu.make_async_remote_copy(
                src_ref=mine.at[s], dst_ref=ten_in.at[s], send_sem=ten_s.at[s], recv_sem=ten_r.at[s],
                device_id={"tensor": ot}, device_id_type=MESH,
            )
            copy.start()
            ten_copies.append(copy)

    bound = len_ref[c]
    lane = lax.broadcasted_iota(jnp.int32, (chunk, LANES), 1)
    slot = lax.broadcasted_iota(jnp.int32, (chunk, LANES), 0)
    total = jnp.zeros((LANES, LANES), jnp.float32)
    for part in range(steps):
        ten_copies[part].wait_recv()
        both = mine[steps + part] + ten_in[part]
        live = jnp.where(slot + part * chunk < bound, both, 0.0)
        right = jnp.where(lane < k, pltpu.roll(both, k, 1), both)
        total += jnp.dot(
            live.T, right, precision=lax.Precision.HIGHEST, preferred_element_type=jnp.float32
        )
    tab[...] = total[0:k] * (seq_len ** -0.5)
    pairs = k // 2
    even = tab[pl.ds(0, pairs, stride=2), :]
    odd = tab[pl.ds(1, pairs, stride=2), :]
    lane2 = lax.broadcasted_iota(jnp.int32, (pairs, LANES), 1)
    flat = jnp.where(lane2 < k, even, odd)
    half = pairs // 2
    flat_ref[0] = flat[0:half]
    flat_ref[1] = flat[half:pairs]

    def sk_copy(to_d, to_c, from_d, from_c, a, e):
        return pltpu.make_async_remote_copy(
            src_ref=flat_ref.at[to_c],
            dst_ref=all_sk.at[pl.ds(pl.multiple_of((from_d * 2 + from_c) * half, half), half)],
            send_sem=sk_s.at[a * 2 + e], recv_sem=sk_r.at[from_d * 2 + from_c],
            device_id={"dp": to_d, "sub": to_c}, device_id_type=MESH,
        )

    pairs_ae = [(a, e) for a in reversed(range(dps)) for e in range(2) if a or e]
    sk_copies = []
    for a, e in pairs_ae:
        copy = sk_copy(lax.rem(d + a, dps), lax.rem(c + e, 2), d, c, a, e)
        copy.start()
        sk_copies.append(copy)
    all_sk[pl.ds(pl.multiple_of((d * 2 + c) * half, half), half)] = flat_ref[c]
    q_load.wait()
    for a, e in reversed(pairs_ae):
        fd, fc = lax.rem(d + dps - a, dps), lax.rem(c + e, 2)
        sk_copy(fd, fc, fd, fc, a, e).wait_recv()

    seqs = 2 * dps
    for m in range(half):
        at = slice(m * LANES, (m + 1) * LANES)
        value = all_sk[pl.ds(m, seqs, stride=half), :]
        first = value.astype(jnp.bfloat16).astype(jnp.float32)
        rest = value - first
        second = rest.astype(jnp.bfloat16).astype(jnp.float32)
        wide[0:seqs, at] = first
        wide[seqs : 2 * seqs, at] = second
        wide[2 * seqs : 3 * seqs, at] = rest - second
        wide[3 * seqs : 4 * seqs, at] = jnp.zeros_like(value)
    prod = lax.dot_general(
        wide[...].astype(jnp.bfloat16), q[...], NT,
        preferred_element_type=jnp.float32,
    )
    part = prod[0:seqs] + prod[seqs : 2 * seqs] + prod[2 * seqs : 3 * seqs]
    rows_q = q.shape[0]
    snd[...] = jnp.zeros_like(snd)
    for to in range(dps):
        snd[to, 0:2, 0:rows_q] = part[2 * to : 2 * to + 2]

    def sc_copy(n, to, sender):
        dd, tt, cc = to
        fd, ft, fc = sender
        slot_of = fd * 4 + ft * 2 + fc
        return pltpu.make_async_remote_copy(
            src_ref=snd.at[dd], dst_ref=rcv.at[slot_of],
            send_sem=sc_s.at[n], recv_sem=sc_r.at[slot_of],
            device_id={"dp": dd, "tensor": tt, "sub": cc}, device_id_type=MESH,
        )

    sc_copies = []
    for n, to in enumerate(reversed(others)):
        copy = sc_copy(n, to, (d, t, c))
        copy.start()
        sc_copies.append(copy)
    rcv[d * 4 + t * 2 + c] = snd[d]

    for e in range(2):
        mine_sk = all_sk[pl.ds(pl.multiple_of((d * 2 + e) * half, half), half), :]
        for m in range(half):
            sk_ref[e : e + 1, m * LANES : (m + 1) * LANES] = mine_sk[m : m + 1, :]

    for n, sender in enumerate(others):
        sc_copy(n, sender, sender).wait_recv()
    for dd in range(dps):
        acc = (rcv[dd * 4] + rcv[dd * 4 + 1]) + (rcv[dd * 4 + 2] + rcv[dd * 4 + 3])
        sc_ref[:, dd * rows_q : (dd + 1) * rows_q] = acc[0:2, 0:rows_q]
    for copy in sub_copies + ten_copies + sk_copies + sc_copies:
        copy.wait_send()


def fused(dps, acts, grads_out, lengths, proj_in, proj_out, query_grads):
    layers, rows, hidden = acts.shape
    model = grads_out.shape[2]
    k = proj_in.shape[2]
    steps = 2
    chunk = SEQ_LEN // steps
    queries, share = query_grads.shape
    half = share // LANES
    ranks = dps * 4
    f32, bf16 = jnp.float32, jnp.bfloat16
    anywhere = pl.BlockSpec(memory_space=pltpu.HBM)
    dma = pltpu.SemaphoreType.DMA
    sketches, scores = pl.pallas_call(
        functools.partial(kernel, dps, chunk, steps),
        out_shape=(
            jax.ShapeDtypeStruct((2, share), f32),
            jax.ShapeDtypeStruct((2, dps * queries), f32),
        ),
        in_specs=[anywhere, anywhere, pl.BlockSpec(memory_space=pltpu.SMEM), anywhere, anywhere, anywhere],
        out_specs=(pl.BlockSpec(memory_space=pltpu.VMEM), pl.BlockSpec(memory_space=pltpu.VMEM)),
        scratch_shapes=[
            pltpu.VMEM((layers, rows, hidden), bf16),
            pltpu.VMEM((layers, rows, model), bf16),
            pltpu.VMEM((layers, k, hidden), bf16),
            pltpu.VMEM((layers, k, model), bf16),
            pltpu.VMEM((queries, share), bf16),
            pltpu.VMEM((2 * steps, chunk, LANES), f32),
            pltpu.VMEM((2 * steps, chunk, LANES), f32),
            pltpu.VMEM((2 * steps, chunk, LANES), f32),
            pltpu.VMEM((steps, chunk, LANES), f32),
            pltpu.VMEM((k, LANES), f32),
            pltpu.VMEM((2, half, LANES), f32),
            pltpu.VMEM((2 * dps * half, LANES), f32),
            pltpu.VMEM((8 * dps, share), f32),
            pltpu.VMEM((dps, 8, LANES), f32),
            pltpu.VMEM((ranks, 8, LANES), f32),
            dma((4 * steps,)), dma((4 * steps,)), dma((2,)), dma((2,)), dma,
            dma((2 * steps,)), dma((2 * steps,)), dma((steps,)), dma((steps,)),
            dma((2 * dps,)), dma((2 * dps,)), dma((ranks,)), dma((ranks,)),
        ],
        compiler_params=pltpu.CompilerParams(
            collective_id=0, has_side_effects=True, vmem_limit_bytes=60 * 1024 * 1024
        ),
    )(acts, grads_out, lengths, proj_in.swapaxes(1, 2), proj_out.swapaxes(1, 2), query_grads)
    return sketches, scores.T


def solution(mesh):
    placed = (
        P(None, ("groups", "dp"), ("tensor", "sub")),
        P(None, ("groups", "dp"), ("tensor", "sub")),
        P(("groups", "dp")),
        P(None, ("tensor", "sub"), None),
        P(None, ("tensor", "sub"), None),
        P("dp", ("tensor", "sub")),
    )

    def body(acts, grads_out, lengths, proj_in, proj_out, query_grads):
        layers, rows, _ = acts.shape
        fits = (
            mesh.shape["tensor"] == 2
            and mesh.shape["sub"] == 2
            and layers == 2
            and lengths.shape[0] == 2
            and rows == 2 * SEQ_LEN
            and 2 * proj_in.shape[2] == LANES
            and query_grads.shape[0] <= LANES
            and 2 * mesh.shape["dp"] == 8
        )
        plan = functools.partial(fused, mesh.shape["dp"]) if fits else per_device
        return plan(acts, grads_out, lengths, proj_in, proj_out, query_grads)

    return jax.shard_map(
        body,
        mesh=mesh,
        in_specs=placed,
        out_specs=(P(("groups", "dp"), ("tensor", "sub")), P(None, ("groups", "dp"))),
        check_vma=False,
    )
```

```python
import functools
import jax
import jax.numpy as jnp
from jax import lax
from jax.experimental import pallas as pl
from jax.experimental.pallas import tpu as pltpu
from jax.sharding import PartitionSpec as P

SEQ_LEN = 512
LANES = 128
MESH = pl.DeviceIdType.MESH
NT = (((1,), (1,)), ((), ()))


def project_side(inputs, weights):
    return jnp.concatenate(
        [
            jnp.dot(inputs[layer], weights[layer], preferred_element_type=jnp.float32)
            for layer in range(inputs.shape[0])
        ],
        axis=1,
    )


def sketch_terms(side_a, side_b, weights, layers):
    rows = side_a.shape[0]
    width = side_a.shape[1] // layers
    left = side_a.reshape(rows, layers, width)
    right = side_b.reshape(rows, layers, width)
    result = jnp.einsum("te,tli,tlj->elij", weights, left, right, precision=lax.Precision.HIGHEST)
    return (result * SEQ_LEN ** (-0.5)).reshape(weights.shape[1], layers * width * width)


def row_weights(lengths, rows, seq_len):
    token = jnp.arange(rows, dtype=jnp.int32)
    seq_of = token // seq_len
    slot = token % seq_len
    owners = jnp.arange(lengths.shape[0], dtype=jnp.int32)
    match = seq_of[:, None] == owners[None, :]
    bound = jnp.sum(jnp.where(match, lengths[None, :], 0), axis=1)
    live = (slot < bound).astype(jnp.float32)
    return match.astype(jnp.float32) * live[:, None]


def per_device(acts, grads_out, lengths, proj_in, proj_out, query_grads):
    layers, rows, _ = acts.shape
    seqs = lengths.shape[0]
    seq_len = rows // seqs
    side_a = project_side(acts, proj_in)
    side_b = project_side(grads_out, proj_out)
    count = lax.axis_size(("tensor", "sub"))
    rank = lax.axis_index(("tensor", "sub"))
    feats = layers * proj_in.shape[2] * proj_in.shape[2]
    share = feats // count
    whole_a, whole_b = lax.psum((side_a, side_b), ("tensor", "sub"))
    weights = row_weights(lengths, rows, seq_len)
    full_sketch = sketch_terms(whole_a, whole_b, weights, layers)
    mine = lax.dynamic_slice_in_dim(full_sketch, rank * share, share, 1)
    block = jnp.dot(
        lax.all_gather(query_grads, "dp", axis=0, tiled=True).astype(jnp.float32),
        mine.T,
        precision=lax.Precision.HIGHEST,
    )
    scores = lax.psum(block, ("tensor", "sub"))
    return (mine, scores)


def kernel(
    dps, chunk, steps,
    x_hbm, g_hbm, len_ref, w_hbm, v_hbm, q_hbm,
    sk_ref, sc_ref,
    x, g, w, v, q, away, mine, sub_in, ten_in, tab, flat_ref, all_sk, wide, snd, rcv,
    x_sem, g_sem, w_sem, v_sem, q_sem,
    sub_s, sub_r, ten_s, ten_r, sk_s, sk_r, sc_s, sc_r,
):
    d = lax.axis_index("dp")
    t = lax.axis_index("tensor")
    c = lax.axis_index("sub")
    ot, oc = 1 - t, 1 - c
    k = w.shape[1]
    seq_len = SEQ_LEN

    items = []
    for layer in (ot, t):
        for part in range(steps):
            for half in (oc, c):
                items.append((layer, half * seq_len + part * chunk))

    def fetch_w(n, layer):
        return (
            pltpu.make_async_copy(w_hbm.at[layer], w.at[layer], w_sem.at[n]),
            pltpu.make_async_copy(v_hbm.at[layer], v.at[layer], v_sem.at[n]),
        )

    def fetch(n):
        layer, row = items[n]
        at = pl.ds(pl.multiple_of(row, chunk), chunk)
        return (
            pltpu.make_async_copy(x_hbm.at[layer, at], x.at[layer, at], x_sem.at[n]),
            pltpu.make_async_copy(g_hbm.at[layer, at], g.at[layer, at], g_sem.at[n]),
        )

    loads = []
    weight_loads = [fetch_w(0, ot), fetch_w(1, t)]
    for n in range(len(items)):
        if n == 0 or n == len(items) // 2:
            for copy in weight_loads[0 if n == 0 else 1]:
                copy.start()
        loads.append(fetch(n))
        for copy in loads[-1]:
            copy.start()
    q_load = pltpu.make_async_copy(q_hbm, q, q_sem)
    q_load.start()

    others = []
    for a in range(dps):
        for b in range(2):
            for e in range(2):
                if a or b or e:
                    others.append((lax.rem(d + a, dps), lax.rem(t + b, 2), lax.rem(c + e, 2)))
    barrier = pltpu.get_barrier_semaphore()
    for dd, tt, cc in others:
        pl.semaphore_signal(
            barrier, inc=1, device_id={"dp": dd, "tensor": tt, "sub": cc}, device_id_type=MESH
        )

    def project(n, out):
        if n == 0 or n == len(items) // 2:
            for copy in weight_loads[0 if n == 0 else 1]:
                copy.wait()
        for copy in loads[n]:
            copy.wait()
        layer, row = items[n]
        at = pl.ds(pl.multiple_of(row, chunk), chunk)
        out[:, 0:k] = lax.dot_general(x[layer, at, :], w[layer], NT, preferred_element_type=jnp.float32)
        out[:, k : 2 * k] = lax.dot_general(g[layer, at, :], v[layer], NT, preferred_element_type=jnp.float32)

    sub_copies, ten_copies = [], []
    for s in range(2 * steps):
        project(2 * s, away.at[s])
        if s == 0:
            pl.semaphore_wait(barrier, len(others))
        copy = pltpu.make_async_remote_copy(
            src_ref=away.at[s], dst_ref=sub_in.at[s], send_sem=sub_s.at[s], recv_sem=sub_r.at[s],
            device_id={"sub": oc}, device_id_type=MESH,
        )
        copy.start()
        sub_copies.append(copy)
        project(2 * s + 1, mine.at[s])
        copy.wait_recv()
        mine[s] += sub_in[s]
        if s < steps:
            copy = pltpu.make_async_remote_copy(
                src_ref=mine.at[s], dst_ref=ten_in.at[s], send_sem=ten_s.at[s], recv_sem=ten_r.at[s],
                device_id={"tensor": ot}, device_id_type=MESH,
            )
            copy.start()
            ten_copies.append(copy)

    bound = len_ref[c]
    lane = lax.broadcasted_iota(jnp.int32, (chunk, LANES), 1)
    slot = lax.broadcasted_iota(jnp.int32, (chunk, LANES), 0)
    total = jnp.zeros((LANES, LANES), jnp.float32)
    for part in range(steps):
        ten_copies[part].wait_recv()
        both = mine[steps + part] + ten_in[part]
        live = jnp.where(slot + part * chunk < bound, both, 0.0)
        right = jnp.where(lane < k, pltpu.roll(both, k, 1), both)
        total += jnp.dot(
            live.T, right, precision=lax.Precision.HIGHEST, preferred_element_type=jnp.float32
        )
    tab[...] = total[0:k] * (seq_len ** -0.5)
    pairs = k // 2
    even = tab[pl.ds(0, pairs, stride=2), :]
    odd = tab[pl.ds(1, pairs, stride=2), :]
    lane2 = lax.broadcasted_iota(jnp.int32, (pairs, LANES), 1)
    flat = jnp.where(lane2 < k, even, odd)
    half = pairs // 2
    flat_ref[0] = flat[0:half]
    flat_ref[1] = flat[half:pairs]

    def sk_copy(to_d, to_c, from_d, from_c, a, e):
        return pltpu.make_async_remote_copy(
            src_ref=flat_ref.at[to_c],
            dst_ref=all_sk.at[pl.ds(pl.multiple_of((from_d * 2 + from_c) * half, half), half)],
            send_sem=sk_s.at[a * 2 + e], recv_sem=sk_r.at[from_d * 2 + from_c],
            device_id={"dp": to_d, "sub": to_c}, device_id_type=MESH,
        )

    pairs_ae = [(a, e) for a in reversed(range(dps)) for e in range(2) if a or e]
    sk_copies = []
    for a, e in pairs_ae:
        copy = sk_copy(lax.rem(d + a, dps), lax.rem(c + e, 2), d, c, a, e)
        copy.start()
        sk_copies.append(copy)
    all_sk[pl.ds(pl.multiple_of((d * 2 + c) * half, half), half)] = flat_ref[c]
    q_load.wait()
    for a, e in reversed(pairs_ae):
        fd, fc = lax.rem(d + dps - a, dps), lax.rem(c + e, 2)
        sk_copy(fd, fc, fd, fc, a, e).wait_recv()

    seqs = 2 * dps
    for m in range(half):
        at = slice(m * LANES, (m + 1) * LANES)
        value = all_sk[pl.ds(m, seqs, stride=half), :]
        first = value.astype(jnp.bfloat16).astype(jnp.float32)
        rest = value - first
        second = rest.astype(jnp.bfloat16).astype(jnp.float32)
        wide[0:seqs, at] = first
        wide[seqs : 2 * seqs, at] = second
        wide[2 * seqs : 3 * seqs, at] = rest - second
        wide[3 * seqs : 4 * seqs, at] = jnp.zeros_like(value)
    prod = lax.dot_general(
        wide[...].astype(jnp.bfloat16), q[...], NT,
        preferred_element_type=jnp.float32,
    )
    part = prod[0:seqs] + prod[seqs : 2 * seqs] + prod[2 * seqs : 3 * seqs]
    rows_q = q.shape[0]
    snd[...] = jnp.zeros_like(snd)
    for to in range(dps):
        snd[to, 0:2, 0:rows_q] = part[2 * to : 2 * to + 2]

    def sc_copy(n, to, sender):
        dd, tt, cc = to
        fd, ft, fc = sender
        slot_of = fd * 4 + ft * 2 + fc
        return pltpu.make_async_remote_copy(
            src_ref=snd.at[dd], dst_ref=rcv.at[slot_of],
            send_sem=sc_s.at[n], recv_sem=sc_r.at[slot_of],
            device_id={"dp": dd, "tensor": tt, "sub": cc}, device_id_type=MESH,
        )

    sc_copies = []
    for n, to in enumerate(reversed(others)):
        copy = sc_copy(n, to, (d, t, c))
        copy.start()
        sc_copies.append(copy)
    rcv[d * 4 + t * 2 + c] = snd[d]

    for e in range(2):
        mine_sk = all_sk[pl.ds(pl.multiple_of((d * 2 + e) * half, half), half), :]
        for m in range(half):
            sk_ref[e : e + 1, m * LANES : (m + 1) * LANES] = mine_sk[m : m + 1, :]

    for n, sender in enumerate(others):
        sc_copy(n, sender, sender).wait_recv()
    for dd in range(dps):
        acc = (rcv[dd * 4] + rcv[dd * 4 + 1]) + (rcv[dd * 4 + 2] + rcv[dd * 4 + 3])
        sc_ref[:, dd * rows_q : (dd + 1) * rows_q] = acc[0:2, 0:rows_q]
    for copy in sub_copies + ten_copies + sk_copies + sc_copies:
        copy.wait_send()


def hand_out(sk_in, sc_in, sk_out, sc_out):
    sk_out[...] = sk_in[...]
    sc_out[...] = sc_in[...]


def fused(dps, acts, grads_out, lengths, proj_in, proj_out, query_grads):
    layers, rows, hidden = acts.shape
    model = grads_out.shape[2]
    k = proj_in.shape[2]
    steps = 2
    chunk = SEQ_LEN // steps
    queries, share = query_grads.shape
    half = share // LANES
    ranks = dps * 4
    f32, bf16 = jnp.float32, jnp.bfloat16
    anywhere = pl.BlockSpec(memory_space=pltpu.HBM)
    dma = pltpu.SemaphoreType.DMA
    sketches, scores = pl.pallas_call(
        functools.partial(kernel, dps, chunk, steps),
        out_shape=(
            jax.ShapeDtypeStruct((2, share), f32),
            jax.ShapeDtypeStruct((2, dps * queries), f32),
        ),
        in_specs=[anywhere, anywhere, pl.BlockSpec(memory_space=pltpu.SMEM), anywhere, anywhere, anywhere],
        out_specs=(pl.BlockSpec(memory_space=pltpu.VMEM), pl.BlockSpec(memory_space=pltpu.VMEM)),
        scratch_shapes=[
            pltpu.VMEM((layers, rows, hidden), bf16),
            pltpu.VMEM((layers, rows, model), bf16),
            pltpu.VMEM((layers, k, hidden), bf16),
            pltpu.VMEM((layers, k, model), bf16),
            pltpu.VMEM((queries, share), bf16),
            pltpu.VMEM((2 * steps, chunk, LANES), f32),
            pltpu.VMEM((2 * steps, chunk, LANES), f32),
            pltpu.VMEM((2 * steps, chunk, LANES), f32),
            pltpu.VMEM((steps, chunk, LANES), f32),
            pltpu.VMEM((k, LANES), f32),
            pltpu.VMEM((2, half, LANES), f32),
            pltpu.VMEM((2 * dps * half, LANES), f32),
            pltpu.VMEM((8 * dps, share), f32),
            pltpu.VMEM((dps, 8, LANES), f32),
            pltpu.VMEM((ranks, 8, LANES), f32),
            dma((4 * steps,)), dma((4 * steps,)), dma((2,)), dma((2,)), dma,
            dma((2 * steps,)), dma((2 * steps,)), dma((steps,)), dma((steps,)),
            dma((2 * dps,)), dma((2 * dps,)), dma((ranks,)), dma((ranks,)),
        ],
        compiler_params=pltpu.CompilerParams(
            collective_id=0, has_side_effects=True, vmem_limit_bytes=60 * 1024 * 1024
        ),
    )(acts, grads_out, lengths, proj_in.swapaxes(1, 2), proj_out.swapaxes(1, 2), query_grads)
    sketches, scores = pl.pallas_call(
        hand_out,
        out_shape=(
            jax.ShapeDtypeStruct(sketches.shape, f32),
            jax.ShapeDtypeStruct(scores.shape, f32),
        ),
    )(sketches, scores)
    return sketches, scores.T


def solution(mesh):
    placed = (
        P(None, ("groups", "dp"), ("tensor", "sub")),
        P(None, ("groups", "dp"), ("tensor", "sub")),
        P(("groups", "dp")),
        P(None, ("tensor", "sub"), None),
        P(None, ("tensor", "sub"), None),
        P("dp", ("tensor", "sub")),
    )

    def body(acts, grads_out, lengths, proj_in, proj_out, query_grads):
        layers, rows, _ = acts.shape
        fits = (
            mesh.shape["tensor"] == 2
            and mesh.shape["sub"] == 2
            and layers == 2
            and lengths.shape[0] == 2
            and rows == 2 * SEQ_LEN
            and 2 * proj_in.shape[2] == LANES
            and query_grads.shape[0] <= LANES
            and 2 * mesh.shape["dp"] == 8
        )
        plan = functools.partial(fused, mesh.shape["dp"]) if fits else per_device
        return plan(acts, grads_out, lengths, proj_in, proj_out, query_grads)

    return jax.shard_map(
        body,
        mesh=mesh,
        in_specs=placed,
        out_specs=(P(("groups", "dp"), ("tensor", "sub")), P(None, ("groups", "dp"))),
        check_vma=False,
    )
```

```python
import functools
import jax
import jax.numpy as jnp
from jax import lax
from jax.experimental import pallas as pl
from jax.experimental.pallas import tpu as pltpu
from jax.sharding import PartitionSpec as P

SEQ_LEN = 512
LANES = 128
MESH = pl.DeviceIdType.MESH
NT = (((1,), (1,)), ((), ()))


def project_side(inputs, weights):
    return jnp.concatenate(
        [
            jnp.dot(inputs[layer], weights[layer], preferred_element_type=jnp.float32)
            for layer in range(inputs.shape[0])
        ],
        axis=1,
    )


def sketch_terms(side_a, side_b, weights, layers):
    rows = side_a.shape[0]
    width = side_a.shape[1] // layers
    left = side_a.reshape(rows, layers, width)
    right = side_b.reshape(rows, layers, width)
    result = jnp.einsum("te,tli,tlj->elij", weights, left, right, precision=lax.Precision.HIGHEST)
    return (result * SEQ_LEN ** (-0.5)).reshape(weights.shape[1], layers * width * width)


def row_weights(lengths, rows, seq_len):
    token = jnp.arange(rows, dtype=jnp.int32)
    seq_of = token // seq_len
    slot = token % seq_len
    owners = jnp.arange(lengths.shape[0], dtype=jnp.int32)
    match = seq_of[:, None] == owners[None, :]
    bound = jnp.sum(jnp.where(match, lengths[None, :], 0), axis=1)
    live = (slot < bound).astype(jnp.float32)
    return match.astype(jnp.float32) * live[:, None]


def per_device(acts, grads_out, lengths, proj_in, proj_out, query_grads):
    layers, rows, _ = acts.shape
    seqs = lengths.shape[0]
    seq_len = rows // seqs
    side_a = project_side(acts, proj_in)
    side_b = project_side(grads_out, proj_out)
    count = lax.axis_size(("tensor", "sub"))
    rank = lax.axis_index(("tensor", "sub"))
    feats = layers * proj_in.shape[2] * proj_in.shape[2]
    share = feats // count
    whole_a, whole_b = lax.psum((side_a, side_b), ("tensor", "sub"))
    weights = row_weights(lengths, rows, seq_len)
    full_sketch = sketch_terms(whole_a, whole_b, weights, layers)
    mine = lax.dynamic_slice_in_dim(full_sketch, rank * share, share, 1)
    block = jnp.dot(
        lax.all_gather(query_grads, "dp", axis=0, tiled=True).astype(jnp.float32),
        mine.T,
        precision=lax.Precision.HIGHEST,
    )
    scores = lax.psum(block, ("tensor", "sub"))
    return (mine, scores)


def kernel(
    dps, chunk, steps,
    x_hbm, g_hbm, len_ref, w_hbm, v_hbm, q_hbm,
    sk_ref, sc_ref,
    x, g, w, v, q, away, mine, sub_in, ten_in, tab, flat_ref, all_sk, wide, snd, rcv,
    x_sem, g_sem, w_sem, v_sem, q_sem,
    sub_s, sub_r, ten_s, ten_r, sk_s, sk_r, sc_s, sc_r,
):
    d = lax.axis_index("dp")
    t = lax.axis_index("tensor")
    c = lax.axis_index("sub")
    ot, oc = 1 - t, 1 - c
    k = w.shape[1]
    seq_len = SEQ_LEN

    items = []
    for layer in (ot, t):
        for part in range(steps):
            for half in (oc, c):
                items.append((layer, half * seq_len + part * chunk))

    def fetch_w(n, layer):
        return (
            pltpu.make_async_copy(w_hbm.at[layer], w.at[layer], w_sem.at[n]),
            pltpu.make_async_copy(v_hbm.at[layer], v.at[layer], v_sem.at[n]),
        )

    def fetch(n):
        layer, row = items[n]
        at = pl.ds(pl.multiple_of(row, chunk), chunk)
        return (
            pltpu.make_async_copy(x_hbm.at[layer, at], x.at[layer, at], x_sem.at[n]),
            pltpu.make_async_copy(g_hbm.at[layer, at], g.at[layer, at], g_sem.at[n]),
        )

    loads = []
    weight_loads = [fetch_w(0, ot), fetch_w(1, t)]
    q_load = pltpu.make_async_copy(q_hbm, q, q_sem)

    def begin(n):
        if n == len(items):
            q_load.start()
        if n >= len(items):
            return
        if n == 0 or n == len(items) // 2:
            for copy in weight_loads[0 if n == 0 else 1]:
                copy.start()
        loads.append(fetch(n))
        for copy in loads[-1]:
            copy.start()

    ahead = 2
    for n in range(ahead):
        begin(n)

    others = []
    for a in range(dps):
        for b in range(2):
            for e in range(2):
                if a or b or e:
                    others.append((lax.rem(d + a, dps), lax.rem(t + b, 2), lax.rem(c + e, 2)))
    barrier = pltpu.get_barrier_semaphore()
    for dd, tt, cc in others:
        pl.semaphore_signal(
            barrier, inc=1, device_id={"dp": dd, "tensor": tt, "sub": cc}, device_id_type=MESH
        )

    def project(n, out):
        if n == 0 or n == len(items) // 2:
            for copy in weight_loads[0 if n == 0 else 1]:
                copy.wait()
        for copy in loads[n]:
            copy.wait()
        begin(n + ahead)
        layer, row = items[n]
        at = pl.ds(pl.multiple_of(row, chunk), chunk)
        out[:, 0:k] = lax.dot_general(x[layer, at, :], w[layer], NT, preferred_element_type=jnp.float32)
        out[:, k : 2 * k] = lax.dot_general(g[layer, at, :], v[layer], NT, preferred_element_type=jnp.float32)

    sub_copies, ten_copies = [], []
    for s in range(2 * steps):
        project(2 * s, away.at[s])
        if s == 0:
            pl.semaphore_wait(barrier, len(others))
        copy = pltpu.make_async_remote_copy(
            src_ref=away.at[s], dst_ref=sub_in.at[s], send_sem=sub_s.at[s], recv_sem=sub_r.at[s],
            device_id={"sub": oc}, device_id_type=MESH,
        )
        copy.start()
        sub_copies.append(copy)
        project(2 * s + 1, mine.at[s])
        copy.wait_recv()
        mine[s] += sub_in[s]
        if s < steps:
            copy = pltpu.make_async_remote_copy(
                src_ref=mine.at[s], dst_ref=ten_in.at[s], send_sem=ten_s.at[s], recv_sem=ten_r.at[s],
                device_id={"tensor": ot}, device_id_type=MESH,
            )
            copy.start()
            ten_copies.append(copy)

    bound = len_ref[c]
    lane = lax.broadcasted_iota(jnp.int32, (chunk, LANES), 1)
    slot = lax.broadcasted_iota(jnp.int32, (chunk, LANES), 0)
    total = jnp.zeros((LANES, LANES), jnp.float32)
    for part in range(steps):
        ten_copies[part].wait_recv()
        both = mine[steps + part] + ten_in[part]
        live = jnp.where(slot + part * chunk < bound, both, 0.0)
        right = jnp.where(lane < k, pltpu.roll(both, k, 1), both)
        total += jnp.dot(
            live.T, right, precision=lax.Precision.HIGHEST, preferred_element_type=jnp.float32
        )
    tab[...] = total[0:k] * (seq_len ** -0.5)
    pairs = k // 2
    even = tab[pl.ds(0, pairs, stride=2), :]
    odd = tab[pl.ds(1, pairs, stride=2), :]
    lane2 = lax.broadcasted_iota(jnp.int32, (pairs, LANES), 1)
    flat = jnp.where(lane2 < k, even, odd)
    half = pairs // 2
    flat_ref[0] = flat[0:half]
    flat_ref[1] = flat[half:pairs]

    def sk_copy(to_d, to_c, from_d, from_c, a, e):
        return pltpu.make_async_remote_copy(
            src_ref=flat_ref.at[to_c],
            dst_ref=all_sk.at[pl.ds(pl.multiple_of((from_d * 2 + from_c) * half, half), half)],
            send_sem=sk_s.at[a * 2 + e], recv_sem=sk_r.at[from_d * 2 + from_c],
            device_id={"dp": to_d, "sub": to_c}, device_id_type=MESH,
        )

    pairs_ae = [(a, e) for a in reversed(range(dps)) for e in range(2) if a or e]
    sk_copies = []
    for a, e in pairs_ae:
        copy = sk_copy(lax.rem(d + a, dps), lax.rem(c + e, 2), d, c, a, e)
        copy.start()
        sk_copies.append(copy)
    all_sk[pl.ds(pl.multiple_of((d * 2 + c) * half, half), half)] = flat_ref[c]
    q_load.wait()
    for a, e in reversed(pairs_ae):
        fd, fc = lax.rem(d + dps - a, dps), lax.rem(c + e, 2)
        sk_copy(fd, fc, fd, fc, a, e).wait_recv()

    seqs = 2 * dps
    for m in range(half):
        at = slice(m * LANES, (m + 1) * LANES)
        value = all_sk[pl.ds(m, seqs, stride=half), :]
        first = value.astype(jnp.bfloat16).astype(jnp.float32)
        rest = value - first
        second = rest.astype(jnp.bfloat16).astype(jnp.float32)
        wide[0:seqs, at] = first
        wide[seqs : 2 * seqs, at] = second
        wide[2 * seqs : 3 * seqs, at] = rest - second
        wide[3 * seqs : 4 * seqs, at] = jnp.zeros_like(value)
    prod = lax.dot_general(
        wide[...].astype(jnp.bfloat16), q[...], NT,
        preferred_element_type=jnp.float32,
    )
    part = prod[0:seqs] + prod[seqs : 2 * seqs] + prod[2 * seqs : 3 * seqs]
    rows_q = q.shape[0]
    snd[...] = jnp.zeros_like(snd)
    for to in range(dps):
        snd[to, 0:2, 0:rows_q] = part[2 * to : 2 * to + 2]

    def sc_copy(n, to, sender):
        dd, tt, cc = to
        fd, ft, fc = sender
        slot_of = fd * 4 + ft * 2 + fc
        return pltpu.make_async_remote_copy(
            src_ref=snd.at[dd], dst_ref=rcv.at[slot_of],
            send_sem=sc_s.at[n], recv_sem=sc_r.at[slot_of],
            device_id={"dp": dd, "tensor": tt, "sub": cc}, device_id_type=MESH,
        )

    sc_copies = []
    for n, to in enumerate(reversed(others)):
        copy = sc_copy(n, to, (d, t, c))
        copy.start()
        sc_copies.append(copy)
    rcv[d * 4 + t * 2 + c] = snd[d]

    for e in range(2):
        mine_sk = all_sk[pl.ds(pl.multiple_of((d * 2 + e) * half, half), half), :]
        for m in range(half):
            sk_ref[e : e + 1, m * LANES : (m + 1) * LANES] = mine_sk[m : m + 1, :]

    for n, sender in enumerate(others):
        sc_copy(n, sender, sender).wait_recv()
    for dd in range(dps):
        acc = (rcv[dd * 4] + rcv[dd * 4 + 1]) + (rcv[dd * 4 + 2] + rcv[dd * 4 + 3])
        sc_ref[:, dd * rows_q : (dd + 1) * rows_q] = acc[0:2, 0:rows_q]
    for copy in sub_copies + ten_copies + sk_copies + sc_copies:
        copy.wait_send()


def hand_out(sk_in, sc_in, sk_out, sc_out):
    sk_out[...] = sk_in[...]
    sc_out[...] = sc_in[...]


def fused(dps, acts, grads_out, lengths, proj_in, proj_out, query_grads):
    layers, rows, hidden = acts.shape
    model = grads_out.shape[2]
    k = proj_in.shape[2]
    steps = 2
    chunk = SEQ_LEN // steps
    queries, share = query_grads.shape
    half = share // LANES
    ranks = dps * 4
    f32, bf16 = jnp.float32, jnp.bfloat16
    anywhere = pl.BlockSpec(memory_space=pltpu.HBM)
    dma = pltpu.SemaphoreType.DMA
    sketches, scores = pl.pallas_call(
        functools.partial(kernel, dps, chunk, steps),
        out_shape=(
            jax.ShapeDtypeStruct((2, share), f32),
            jax.ShapeDtypeStruct((2, dps * queries), f32),
        ),
        in_specs=[anywhere, anywhere, pl.BlockSpec(memory_space=pltpu.SMEM), anywhere, anywhere, anywhere],
        out_specs=(pl.BlockSpec(memory_space=pltpu.VMEM), pl.BlockSpec(memory_space=pltpu.VMEM)),
        scratch_shapes=[
            pltpu.VMEM((layers, rows, hidden), bf16),
            pltpu.VMEM((layers, rows, model), bf16),
            pltpu.VMEM((layers, k, hidden), bf16),
            pltpu.VMEM((layers, k, model), bf16),
            pltpu.VMEM((queries, share), bf16),
            pltpu.VMEM((2 * steps, chunk, LANES), f32),
            pltpu.VMEM((2 * steps, chunk, LANES), f32),
            pltpu.VMEM((2 * steps, chunk, LANES), f32),
            pltpu.VMEM((steps, chunk, LANES), f32),
            pltpu.VMEM((k, LANES), f32),
            pltpu.VMEM((2, half, LANES), f32),
            pltpu.VMEM((2 * dps * half, LANES), f32),
            pltpu.VMEM((8 * dps, share), f32),
            pltpu.VMEM((dps, 8, LANES), f32),
            pltpu.VMEM((ranks, 8, LANES), f32),
            dma((4 * steps,)), dma((4 * steps,)), dma((2,)), dma((2,)), dma,
            dma((2 * steps,)), dma((2 * steps,)), dma((steps,)), dma((steps,)),
            dma((2 * dps,)), dma((2 * dps,)), dma((ranks,)), dma((ranks,)),
        ],
        compiler_params=pltpu.CompilerParams(
            collective_id=0, has_side_effects=True, vmem_limit_bytes=60 * 1024 * 1024
        ),
    )(acts, grads_out, lengths, proj_in.swapaxes(1, 2), proj_out.swapaxes(1, 2), query_grads)
    sketches, scores = pl.pallas_call(
        hand_out,
        out_shape=(
            jax.ShapeDtypeStruct(sketches.shape, f32),
            jax.ShapeDtypeStruct(scores.shape, f32),
        ),
    )(sketches, scores)
    return sketches, scores.T


def solution(mesh):
    placed = (
        P(None, ("groups", "dp"), ("tensor", "sub")),
        P(None, ("groups", "dp"), ("tensor", "sub")),
        P(("groups", "dp")),
        P(None, ("tensor", "sub"), None),
        P(None, ("tensor", "sub"), None),
        P("dp", ("tensor", "sub")),
    )

    def body(acts, grads_out, lengths, proj_in, proj_out, query_grads):
        layers, rows, _ = acts.shape
        fits = (
            mesh.shape["tensor"] == 2
            and mesh.shape["sub"] == 2
            and layers == 2
            and lengths.shape[0] == 2
            and rows == 2 * SEQ_LEN
            and 2 * proj_in.shape[2] == LANES
            and query_grads.shape[0] <= LANES
            and 2 * mesh.shape["dp"] == 8
        )
        plan = functools.partial(fused, mesh.shape["dp"]) if fits else per_device
        return plan(acts, grads_out, lengths, proj_in, proj_out, query_grads)

    return jax.shard_map(
        body,
        mesh=mesh,
        in_specs=placed,
        out_specs=(P(("groups", "dp"), ("tensor", "sub")), P(None, ("groups", "dp"))),
        check_vma=False,
    )
```
